32 devices in a mesh: dp: 4 (over z), row: 2 (over x), col: 4 (over y, core).
Axes of the slice: x: 2, y: 2, z: 4, core: 2. Of those that a mesh axis runs over, the one named last changes fastest.
Arguments:
- inputs: float32 [1024, 6144], P('dp', 'row'), may hold values from -6 to 6
- out_grad: float32 [1024, 2048], P('dp', 'col'), may hold values from -6 to 6
- weight: float32 [6144, 2048], P(('row', 'dp'), 'col'), may hold values from -0.078125 to 0.078125
- moment_mean: float32 [6144, 2048], P(('row', 'dp'), 'col'), may hold values from -6 to 6
- moment_square: float32 [6144, 2048], P(('row', 'dp'), 'col'), may hold values from 0.5 to 2
Outputs:
- outputs: float32 [1024, 2048], P(('dp', 'row'), 'col')
- in_grad: float32 [1024, 6144], P(('dp', 'col'), 'row')
- new_weight: float32 [6144, 2048], P(('row', 'dp'), 'col')
- new_mean: float32 [6144, 2048], P(('row', 'dp'), 'col')
- new_square: float32 [6144, 2048], P(('row', 'dp'), 'col')
The draws below stay inside these ranges and needn't reach their ends.
All inputs are finite; a program needn't handle non-finite values.
Results may differ from the reference program's by a relative error of at most 0.00007.
Values sent between devices are 32-bit elements; how exact they have to be, the bound alone decides.
No kernel may reach another device: no remote copies, remote signals or barrier semaphores. Data moves between devices by JAX's collectives and lax.ppermute only.
A program may use at most 64 MiB of HBM per device.

```python
import math
import jax
import jax.numpy as jnp
from jax import lax

DIN = 6144
DOUT = 2048
STEP = 10
TOKENS = 1024


def block_scale(stream_key, dims, pieces, least, largest):
    loudness = 1.0
    for axis_at, parts in pieces:
        steps = jax.random.uniform(jax.random.fold_in(jax.random.fold_in(stream_key, 6), axis_at), (parts,), jnp.float32, least / len(pieces), largest / len(pieces))
        loudness = loudness * jnp.repeat(jnp.exp(steps), dims[axis_at] // parts).reshape((-1,) + (1,) * (len(dims) - 1 - axis_at))
    return loudness


def normal_values(rng, extent, spread, reach, pieces=(), held_as=jnp.bfloat16):
    array = spread * jax.random.normal(rng, extent, jnp.float32)
    if pieces:
        array = array * block_scale(rng, extent, pieces, -0.22, 0.18)
    return jnp.clip(array, -reach, reach).astype(held_as)


def setup_inputs(seed: int = 0) -> dict:
    key_list = jax.random.split(jax.random.key(seed), 6)
    return {
        "inputs": normal_values(key_list[0], (TOKENS, DIN), 1.0, 6.0, ((0, 4), (1, 2)), jnp.float32),
        "out_grad": normal_values(key_list[1], (TOKENS, DOUT), 1.0, 6.0, ((0, 4), (1, 4)), jnp.float32),
        "weight": normal_values(key_list[2], (DIN, DOUT), DIN ** -0.5, 0.078125, ((0, 8), (1, 4)), jnp.float32),
        "moment_mean": normal_values(key_list[3], (DIN, DOUT), 1.0, 6.0, ((0, 8), (1, 4)), jnp.float32),
        "moment_square": jnp.clip(jnp.exp(math.log(2.0) - 1.3862944 * jax.random.uniform(key_list[4], (DIN, DOUT), jnp.float32) ** block_scale(key_list[4], (DIN, DOUT), ((0, 8), (1, 4)), -0.2, 0.2)), 0.5, 2.0),
    }


def adamw_update(weight, moment_mean, moment_square, gradient):
    new_mean = 0.9 * moment_mean + 0.1 * gradient
    new_square = 0.95 * moment_square + 0.05 * gradient * gradient
    mean_hat = new_mean / (1.0 - 0.9 ** STEP)
    square_hat = new_square / (1.0 - 0.95 ** STEP)
    new_weight = weight - 0.02 * (mean_hat / (jnp.sqrt(square_hat) + 1e-08) + 0.1 * weight)
    return (new_weight, new_mean, new_square)

def reference(inputs, out_grad, weight, moment_mean, moment_square):
    highest = lax.Precision.HIGHEST
    outputs = jnp.dot(inputs, weight, precision=highest, preferred_element_type=jnp.float32)
    in_grad = lax.dot_general(out_grad, weight, (((1,), (1,)), ((), ())), precision=highest, preferred_element_type=jnp.float32)
    gradient = lax.dot_general(inputs, out_grad, (((0,), (0,)), ((), ())), precision=highest, preferred_element_type=jnp.float32)
    gradient = gradient * (1.0 / math.sqrt(TOKENS))
    new_weight, new_mean, new_square = adamw_update(weight, moment_mean, moment_square, gradient)
    return (outputs, in_grad, new_weight, new_mean, new_square)
```

```python
import functools
import math

import jax
import jax.numpy as jnp
from jax import lax
from jax.experimental import pallas as pl
from jax.experimental.pallas import tpu as pltpu
from jax.sharding import PartitionSpec as P

STEP = 10
F32 = jnp.float32
BF16 = jnp.bfloat16
VMEM = pl.BlockSpec(memory_space=pltpu.VMEM)
HBM = pl.BlockSpec(memory_space=pl.ANY)
NN = (((1,), (0,)), ((), ()))
NT = (((1,), (1,)), ((), ()))
TN = (((0,), (0,)), ((), ()))


def adamw_update(weight, moment_mean, moment_square, gradient):
    new_mean = 0.9 * moment_mean + 0.1 * gradient
    new_square = 0.95 * moment_square + 0.05 * gradient * gradient
    mean_hat = new_mean / (1.0 - 0.9**STEP)
    square_hat = new_square / (1.0 - 0.95**STEP)
    new_weight = weight - 0.02 * (mean_hat / (jnp.sqrt(square_hat) + 1e-08) + 0.1 * weight)
    return (new_weight, new_mean, new_square)


def gather_weight(inputs, out_grad, weight, moment_mean, moment_square):
    highest = lax.Precision.HIGHEST
    whole = lax.all_gather(weight, "dp", axis=0, tiled=True)
    partial_out = jnp.dot(inputs, whole, precision=highest, preferred_element_type=F32)
    partial_in = lax.dot_general(out_grad, whole, NT, precision=highest, preferred_element_type=F32)
    outputs = lax.psum_scatter(partial_out, "row", scatter_dimension=0, tiled=True)
    in_grad = lax.psum_scatter(partial_in, "col", scatter_dimension=0, tiled=True)
    factor = 1.0 / math.sqrt(inputs.shape[0] * lax.axis_size("dp"))
    product = lax.dot_general(inputs, out_grad, TN, precision=highest, preferred_element_type=F32)
    gradient = lax.psum_scatter(product, "dp", scatter_dimension=0, tiled=True) * factor
    return (outputs, in_grad, *adamw_update(weight, moment_mean, moment_square, gradient))


def halves(x):
    hi = x.astype(BF16)
    return hi, (x - hi.astype(F32)).astype(BF16)


def dot3(a, b, dims):
    f = functools.partial(lax.dot_general, dimension_numbers=dims, preferred_element_type=F32)
    return f(a[0], b[0]) + (f(a[0], b[1]) + f(a[1], b[0]))


def call(kernel, ins, outs, flops=0, scratch=(), in_spec=VMEM, limit=48 << 20):
    moved = sum(math.prod(a.shape) * a.dtype.itemsize for a in (*ins, *outs))
    return pl.pallas_call(
        kernel,
        out_shape=tuple(jax.ShapeDtypeStruct(o.shape, o.dtype) for o in outs),
        in_specs=[in_spec] * len(ins),
        out_specs=tuple([VMEM] * len(outs)),
        scratch_shapes=list(scratch),
        compiler_params=pltpu.CompilerParams(vmem_limit_bytes=limit),
        cost_estimate=pl.CostEstimate(flops=flops, bytes_accessed=moved // 4, transcendentals=0),
    )(*ins)


def f32(*shape):
    return jax.ShapeDtypeStruct(shape, F32)


def b16(*shape):
    return jax.ShapeDtypeStruct(shape, BF16)


def doubling(n):
    bits, order = [], [0]
    while 1 << len(bits) < n:
        bits.insert(0, 1 << len(bits))
    for bit in bits:
        order = order + [o ^ bit for o in order]
    return bits, order


def swap(x, axis, bit):
    n = lax.axis_size(axis)
    return lax.ppermute(x, axis, [(i, i ^ bit) for i in range(n)])


def keep_weight(inputs, out_grad, weight, moment_mean, moment_square):
    dp, row, col = (lax.axis_size(a) for a in ("dp", "row", "col"))
    tokens, rows, cols = inputs.shape[0], weight.shape[0], weight.shape[1]
    slab, half, part = tokens // col, tokens // row, tokens // 2
    col_bits, order = doubling(col)
    flops = 6 * tokens * rows * cols

    def send_g(g_ref, o_ref, sem):
        r, c = lax.axis_index("row"), lax.axis_index("col")
        n = col // row
        copies = []
        for j in range(n):
            at = order[j]
            for q in range(1, row):
                at = jnp.where(r == q, order[q * n + j], at)
            src = g_ref.at[pl.ds(pl.multiple_of((c ^ at) * slab, slab), slab), :]
            copies.append(pltpu.make_async_copy(src, o_ref.at[pl.ds(j * slab, slab), :], sem.at[j]))
        for cp in copies:
            cp.start()
        for cp in copies:
            cp.wait()

    (g_half,) = call(send_g, [out_grad], [f32(half, cols)], in_spec=HBM, scratch=[pltpu.SemaphoreType.DMA((col // row,))])

    def send_x(x_ref, *refs):
        outs, sem = refs[:-1], refs[-1]
        d, c = lax.axis_index("dp"), lax.axis_index("col")
        copies = []
        for k in range(1, dp):
            src = x_ref.at[pl.ds(pl.multiple_of(c * slab, slab), slab), pl.ds(pl.multiple_of((d ^ k) * rows, rows), rows)]
            copies.append(pltpu.make_async_copy(src, outs[k - 1], sem.at[k - 1]))
        for cp in copies:
            cp.start()
        for cp in copies:
            cp.wait()

    x_send = call(send_x, [inputs], [f32(slab, rows)] * (dp - 1), in_spec=HBM, scratch=[pltpu.SemaphoreType.DMA((dp - 1,))])

    dp_bits, _ = doubling(dp)
    g_mine = {0: g_half}
    stages = []
    for bit in dp_bits:
        ks = sorted(g_mine)
        sent = g_half if len(ks) == 1 else jnp.concatenate([g_mine[k] for k in ks], axis=0)
        got = swap(sent, "dp", bit)
        for i, k in enumerate(ks):
            g_mine[k ^ bit] = got[i * half : (i + 1) * half]
        stages.append(([k ^ bit for k in ks], got))

    x_block = {}
    for k in range(1, dp):
        piece = swap(x_send[k - 1], "dp", k)
        for bit in col_bits:
            piece = jnp.concatenate([piece, swap(piece, "col", bit)], axis=0)
        x_block[k] = piece

    def own(x_ref, g_ref, w_ref, wh_ref, wl_ref, xo_ref, go_ref, sem):
        d, c = lax.axis_index("dp"), lax.axis_index("col")
        copies = []
        for j in range(col):
            at = pl.ds(pl.multiple_of((c ^ order[j]) * slab, slab), slab)
            to = pl.ds(j * slab, slab)
            copies.append(pltpu.make_async_copy(x_ref.at[at, pl.ds(pl.multiple_of(d * rows, rows), rows)], xo_ref.at[to, :], sem.at[2 * j]))
            copies.append(pltpu.make_async_copy(g_ref.at[at, :], go_ref.at[to, :], sem.at[2 * j + 1]))
        for cp in copies:
            cp.start()
        wh_ref[...], wl_ref[...] = halves(w_ref[...])
        for cp in copies:
            cp.wait()

    w_hi, w_lo, x_own, g_own = pl.pallas_call(
        own,
        out_shape=(b16(rows, cols), b16(rows, cols), f32(tokens, rows), f32(tokens, cols)),
        in_specs=[HBM, HBM, VMEM],
        out_specs=(VMEM,) * 4,
        scratch_shapes=[pltpu.SemaphoreType.DMA((2 * col,))],
        compiler_params=pltpu.CompilerParams(vmem_limit_bytes=48 << 20),
        cost_estimate=pl.CostEstimate(flops=0, bytes_accessed=4 << 20, transcendentals=0),
    )(inputs, out_grad, weight)
    x_block[0] = x_own

    def in_kernel(n_own, n, *refs):
        g, (wh, wl, keep, send) = refs[: n_own + 2 * n], refs[n_own + 2 * n :]
        w = (wh[...], wl[...])
        r = lax.axis_index("row")
        for i in range(n_own):
            p = dot3(halves(g[i][...]), w, NT)
            keep[i], send[i] = p[:part], p[part:]
        for i in range(n):
            a, b = g[n_own + 2 * i][...], g[n_own + 2 * i + 1][...]
            first = jnp.where(r == 0, a, b)
            second = jnp.where(r == 0, b, a)
            j = n_own + i
            keep[j] = dot3(halves(first), w, NT)
            send[j] = dot3(halves(second), w, NT)

    def in_partial(own_blocks, pairs):
        n = len(own_blocks) + len(pairs)
        flat = [*own_blocks, *(a for pair in pairs for a in pair)]
        return call(functools.partial(in_kernel, len(own_blocks), len(pairs)), [*flat, w_hi, w_lo],
                    [f32(n, part, rows)] * 2, flops=n * flops)

    def reduce_col(keep, send):
        n, size = keep.shape[0], part
        for bit in reversed(col_bits):
            total = keep + swap(send, "col", bit)
            size //= 2
            keep, send = total[:, :size], total[:, size:]
        return total

    def reduce_in(keep, send):
        total = keep + swap(send, "col", col_bits[-1])
        return total[:, :slab] + swap(total[:, slab:], "col", col_bits[0])

    g_pair = {}
    in_total = {}
    for ks, got in stages:
        other = swap(got, "row", 1)
        for i, k in enumerate(ks):
            g_pair[k] = (got[i * half : (i + 1) * half], other[i * half : (i + 1) * half])
        group = ([0] if ks[0] == dp_bits[0] else []) + ks
        total = reduce_in(*in_partial([g_own] if 0 in group else [], [g_pair[k] for k in ks]))
        for i, k in enumerate(group):
            in_total[k] = total[i]

    in_grad = jnp.zeros((slab, dp * rows), F32)
    d = lax.axis_index("dp")
    for k in range(dp):
        piece = in_total[k] if k == 0 else swap(in_total[k], "dp", k)
        in_grad = lax.dynamic_update_slice(in_grad, piece, (0, (d ^ k) * rows))

    def out_kernel(n, *refs):
        xs, (wh, wl, keep, send) = refs[:n], refs[n:]
        w = (wh[...], wl[...])
        kept = (lax.axis_index("col") // (col // row)) ^ lax.axis_index("row")
        for i in range(n):
            o = dot3(halves(xs[i][...]), w, NN)
            for j in range(col // row):
                a, b = o[2 * j * slab : (2 * j + 1) * slab], o[(2 * j + 1) * slab : (2 * j + 2) * slab]
                keep[i, j * slab : (j + 1) * slab, :] = jnp.where(kept == 0, a, b)
                send[i, j * slab : (j + 1) * slab, :] = jnp.where(kept == 0, b, a)

    def out_partial(ks):
        n = len(ks)
        keep, send = call(functools.partial(out_kernel, n), [*(x_block[k] for k in ks), w_hi, w_lo],
                          [f32(n, half, cols)] * 2, flops=n * flops)
        return keep + swap(send, "row", 1)

    odd = out_partial([1, 3])
    even = out_partial([0, 2])
    even = even + swap(odd, "dp", 1)
    out = even[0] + swap(even[1], "dp", 2)
    low = lax.axis_index("col") % 2
    outputs = jnp.where(low == 0, out, jnp.concatenate([out[slab:], out[:slab]], axis=0))

    factor = 1.0 / math.sqrt(tokens * dp)

    def grad_kernel(*refs):
        xs = refs[:dp]
        g0, gs = refs[dp], refs[dp + 1 : 3 * dp - 1]
        w, m, v, nw, nm, nv = refs[3 * dp - 1 :]
        r = lax.axis_index("row")
        total = dot3(halves(xs[0][...]), halves(g0[...]), TN)
        for k in range(1, dp):
            a, b = gs[2 * (k - 1)][...], gs[2 * (k - 1) + 1][...]
            g = jnp.concatenate([jnp.where(r == 0, a, b), jnp.where(r == 0, b, a)], axis=0)
            total = total + dot3(halves(xs[k][...]), halves(g), TN)
        nw[...], nm[...], nv[...] = adamw_update(w[...], m[...], v[...], total * factor)

    new_weight, new_mean, new_square = call(
        grad_kernel,
        [*(x_block[k] for k in range(dp)), g_own, *(a for k in range(1, dp) for a in g_pair[k]), weight, moment_mean, moment_square],
        [f32(rows, cols)] * 3,
        flops=dp * flops,
    )
    return (outputs, in_grad, new_weight, new_mean, new_square)


def solution(mesh):
    specs = (P("dp", "row"), P("dp", "col"), *[P(("row", "dp"), "col")] * 3)
    out_specs = (P(("dp", "row"), "col"), P(("dp", "col"), "row"), *[P(("row", "dp"), "col")] * 3)

    def step(inputs, out_grad, weight, moment_mean, moment_square):
        dp, row, col = (mesh.shape[a] for a in ("dp", "row", "col"))
        tokens = inputs.shape[0] // dp
        rows, cols = weight.shape[0] // (row * dp), weight.shape[1] // col
        pairs = dp == 4 and row == 2 and col == 4
        lighter = tokens * (rows // col + cols // row) < rows * cols
        plan = keep_weight if pairs and lighter else gather_weight
        return jax.shard_map(plan, mesh=mesh, in_specs=specs, out_specs=out_specs, check_vma=False)(
            inputs, out_grad, weight, moment_mean, moment_square
        )

    return step
```

```python
import functools
import math

import jax
import jax.numpy as jnp
from jax import lax
from jax.experimental import pallas as pl
from jax.experimental.pallas import tpu as pltpu
from jax.sharding import PartitionSpec as P

STEP = 10
F32 = jnp.float32
BF16 = jnp.bfloat16
VMEM = pl.BlockSpec(memory_space=pltpu.VMEM)
HBM = pl.BlockSpec(memory_space=pltpu.HBM)
NN = (((1,), (0,)), ((), ()))
NT = (((1,), (1,)), ((), ()))
TN = (((0,), (0,)), ((), ()))


def adamw_update(weight, moment_mean, moment_square, gradient):
    new_mean = 0.9 * moment_mean + 0.1 * gradient
    new_square = 0.95 * moment_square + 0.05 * gradient * gradient
    mean_hat = new_mean / (1.0 - 0.9**STEP)
    square_hat = new_square / (1.0 - 0.95**STEP)
    new_weight = weight - 0.02 * (mean_hat / (jnp.sqrt(square_hat) + 1e-08) + 0.1 * weight)
    return (new_weight, new_mean, new_square)


ORDER = " ".join(
    (
        "sg sx b1 own",
        "b2 in1 a1 a3",
        "out0 in2 a2 b3",
        "in0 ay1 cx0 ay3",
        "dc2 out1 out3 in3",
        "ay2 dy2 dc1 cx3",
        "dc0 dc3 out2 dz2",
        "dy3 cx1 c2 dz3",
        "dy1 grad fin dz1",
        "dy0",
    )
)
HOLD = {"B3": "in1", "B2": "sx", "A3": "b1", "Dc1": "a3", "Dy1": "cx1", "Cx3": "out1", "A1": "b1"}


def gather_weight(inputs, out_grad, weight, moment_mean, moment_square):
    highest = lax.Precision.HIGHEST
    whole = lax.all_gather(weight, "dp", axis=0, tiled=True)
    partial_out = jnp.dot(inputs, whole, precision=highest, preferred_element_type=F32)
    partial_in = lax.dot_general(out_grad, whole, NT, precision=highest, preferred_element_type=F32)
    outputs = lax.psum_scatter(partial_out, "row", scatter_dimension=0, tiled=True)
    in_grad = lax.psum_scatter(partial_in, "col", scatter_dimension=0, tiled=True)
    factor = 1.0 / math.sqrt(inputs.shape[0] * lax.axis_size("dp"))
    product = lax.dot_general(inputs, out_grad, TN, precision=highest, preferred_element_type=F32)
    gradient = lax.psum_scatter(product, "dp", scatter_dimension=0, tiled=True) * factor
    return (outputs, in_grad, *adamw_update(weight, moment_mean, moment_square, gradient))


def halves(x):
    hi = x.astype(BF16)
    return hi, (x - hi.astype(F32)).astype(BF16)


def dot3(a, b, dims):
    f = functools.partial(lax.dot_general, dimension_numbers=dims, preferred_element_type=F32)
    return f(a[0], b[0]) + (f(a[0], b[1]) + f(a[1], b[0]))


def call(kernel, ins, outs, scratch=(), far=0, far_outs=0, limit=16 << 20):
    ins = [pltpu.with_memory_space_constraint(a, pltpu.HBM) if i < far else a for i, a in enumerate(ins)]
    return pl.pallas_call(
        kernel,
        out_shape=tuple(pltpu.HBM(o.shape, o.dtype) if i < far_outs else o for i, o in enumerate(outs)),
        in_specs=[HBM if i < far else VMEM for i in range(len(ins))],
        out_specs=tuple(HBM if i < far_outs else VMEM for i in range(len(outs))),
        scratch_shapes=list(scratch),
        compiler_params=pltpu.CompilerParams(vmem_limit_bytes=limit),
        cost_estimate=pl.CostEstimate(flops=1000, bytes_accessed=1000, transcendentals=0),
    )(*ins)


def f32(*shape):
    return jax.ShapeDtypeStruct(shape, F32)


def b16(*shape):
    return jax.ShapeDtypeStruct(shape, BF16)


def doubling(n):
    bits, order = [], [0]
    while 1 << len(bits) < n:
        bits.insert(0, 1 << len(bits))
    for bit in bits:
        order = order + [o ^ bit for o in order]
    return bits, order


def swap(x, axis, bit):
    n = lax.axis_size(axis)
    return lax.ppermute(x, axis, [(i, i ^ bit) for i in range(n)])


def keep_weight(inputs, out_grad, weight, moment_mean, moment_square):
    dp, row, col = (lax.axis_size(a) for a in ("dp", "row", "col"))
    tokens, rows, cols = inputs.shape[0], weight.shape[0], weight.shape[1]
    slab, half, part = tokens // col, tokens // row, tokens // 2
    col_bits, order = doubling(col)
    near, far = col_bits[1], col_bits[0]
    last = []

    def after(*xs):
        out = lax.optimization_barrier((*xs, *last))[: len(xs)] if last else xs
        return out[0] if len(xs) == 1 else out

    def mark(*ys):
        last[:] = ys

    def send_g(g_ref, o_ref, sem):
        r, c = lax.axis_index("row"), lax.axis_index("col")
        n = col // row
        copies = []
        for j in range(n):
            at = order[j]
            for q in range(1, row):
                at = jnp.where(r == q, order[q * n + j], at)
            src = g_ref.at[pl.ds(pl.multiple_of((c ^ at) * slab, slab), slab), :]
            copies.append(pltpu.make_async_copy(src, o_ref.at[pl.ds(j * slab, slab), :], sem.at[j]))
        for cp in copies:
            cp.start()
        for cp in copies:
            cp.wait()

    def send_x(x_ref, *refs):
        outs, sem = refs[:-1], refs[-1]
        d, c = lax.axis_index("dp"), lax.axis_index("col")
        copies = []
        for k in range(1, dp):
            src = x_ref.at[pl.ds(pl.multiple_of(c * slab, slab), slab), pl.ds(pl.multiple_of((d ^ k) * rows, rows), rows)]
            copies.append(pltpu.make_async_copy(src, outs[k - 1], sem.at[k - 1]))
        for cp in copies:
            cp.start()
        for cp in copies:
            cp.wait()

    def own(x_ref, g_ref, w_ref, wh_ref, wl_ref, xo_ref, go_ref, sem):
        d, c = lax.axis_index("dp"), lax.axis_index("col")
        copies = []
        for j in range(col):
            at = pl.ds(pl.multiple_of((c ^ order[j]) * slab, slab), slab)
            to = pl.ds(j * slab, slab)
            copies.append(pltpu.make_async_copy(x_ref.at[at, pl.ds(pl.multiple_of(d * rows, rows), rows)], xo_ref.at[to, :], sem.at[2 * j]))
            copies.append(pltpu.make_async_copy(g_ref.at[at, :], go_ref.at[to, :], sem.at[2 * j + 1]))
        for cp in copies:
            cp.start()
        wh_ref[...], wl_ref[...] = halves(w_ref[...])
        for cp in copies:
            cp.wait()

    def in_kernel(*refs):
        g, (wh, wl, keep, send) = refs[:-4], refs[-4:]
        w = (wh[...], wl[...])
        if len(g) == 1:
            first, second = g[0][:part], g[0][part:]
        else:
            r = lax.axis_index("row")
            a, b = g[0][...], g[1][...]
            first, second = jnp.where(r == 0, a, b), jnp.where(r == 0, b, a)
        keep[...] = dot3(halves(first), w, NT)
        send[...] = dot3(halves(second), w, NT)

    def in_block(*g):
        return call(in_kernel, [*g, w_hi, w_lo], [f32(part, rows)] * 2)

    def out_kernel(*refs):
        xs, (wh, wl, keep, send) = refs[:-4], refs[-4:]
        w = (wh[...], wl[...])
        kept = (lax.axis_index("col") // (col // row)) ^ lax.axis_index("row")
        x = xs[0][...] if len(xs) == 1 else jnp.concatenate([x[...] for x in xs], axis=0)
        o = dot3(halves(x), w, NN)
        for j in range(col // row):
            a, b = o[2 * j * slab : (2 * j + 1) * slab], o[(2 * j + 1) * slab : (2 * j + 2) * slab]
            keep[j * slab : (j + 1) * slab, :] = jnp.where(kept == 0, a, b)
            send[j * slab : (j + 1) * slab, :] = jnp.where(kept == 0, b, a)

    def out_block(*x):
        return call(out_kernel, [*x, w_hi, w_lo], [f32(half, cols)] * 2)

    factor = 1.0 / math.sqrt(tokens * dp)

    def grad_kernel(*refs):
        n = 4 * dp - 2
        blocks, moments, outs = refs[:n], refs[n : n + 3], refs[n + 3 : n + 6]
        x_at, g_at, state, total, sem, state_sem, out_sem = refs[n + 6 :]
        r = lax.axis_index("row")
        copies = []
        for k in range(dp):
            if k == 0:
                pieces = [(blocks[0], x_at, 0, 0, tokens), (blocks[2 * dp - 1], g_at, 0, 0, tokens)]
            else:
                pieces = [(blocks[2 * k - 1 + i], x_at, k, i * part, part) for i in range(2)]
                pieces += [(blocks[2 * dp - 2 + 2 * k + i], g_at, k, (r ^ i) * half, half) for i in range(2)]
            for i, (src, to, q, start, size) in enumerate(pieces):
                start = start if isinstance(start, int) else pl.multiple_of(start, size)
                copies.append((k, pltpu.make_async_copy(src, to.at[q, pl.ds(start, size), :], sem.at[4 * k + i])))
        states = [pltpu.make_async_copy(m, state.at[i], state_sem.at[i]) for i, m in enumerate(moments)]
        for _, cp in copies:
            cp.start()
        for cp in states:
            cp.start()
        for k in range(dp):
            for q, cp in copies:
                if q == k:
                    cp.wait()
            add = dot3(halves(x_at[k]), halves(g_at[k]), TN)
            total[...] = add if k == 0 else total[...] + add
        for cp in states:
            cp.wait()
        sends = []
        size = rows // 4
        for i in range(4):
            at = pl.ds(i * size, size)
            new = adamw_update(state[0, at, :], state[1, at, :], state[2, at, :], total[at, :] * factor)
            for q in range(3):
                state[q, at, :] = new[q]
                sends.append(pltpu.make_async_copy(state.at[q, at, :], outs[q].at[at, :], out_sem.at[3 * i + q]))
                sends[-1].start()
        for cp in sends:
            cp.wait()

    permutes = {"B2": ("dp", 2), "B1": ("dp", 1), "B3": ("dp", 1), "C1": ("dp", 1), "C3": ("dp", 1), "C2": ("dp", 2)}
    for k in range(dp):
        permutes |= {f"A{k}": ("dp", k), f"Dz{k}": ("dp", k), f"Bx{k}": ("row", 1), f"Cx{k}": ("row", 1)}
        permutes |= {f"Ay{k}": ("col", far), f"Ac{k}": ("col", near), f"Dy{k}": ("col", far), f"Dc{k}": ("col", near)}
    ready, sent, got, v = {}, {}, {}, {}

    def take(name):
        return after(got[name])

    def give(name, x):
        ready[name] = x

    def step_sg():
        (v["g"],) = call(send_g, [out_grad], [f32(half, cols)], far=1, scratch=[pltpu.SemaphoreType.DMA((col // row,))])
        give("B2", v["g"])
        give("B1", v["g"])
        return v["g"]

    def step_sx():
        xs = call(send_x, [after(inputs)], [f32(slab, rows)] * (dp - 1), far=1, scratch=[pltpu.SemaphoreType.DMA((dp - 1,))])
        for k in range(1, dp):
            give(f"A{k}", xs[k - 1])
        return xs[0]

    def step_own():
        v["wh"], v["wl"], v["x0"], v["g0"] = call(
            own,
            [after(inputs), out_grad, weight],
            [b16(rows, cols), b16(rows, cols), f32(tokens, rows), f32(tokens, cols)],
            far=2,
            scratch=[pltpu.SemaphoreType.DMA((2 * col,))],
        )
        return v["wh"]

    def step_b(k):
        v[f"g{k}"] = take(f"B{k}")
        if k == 2:
            give("B3", v["g2"])
        give(f"Bx{k}", v[f"g{k}"])
        return v[f"g{k}"]

    def step_in(k):
        if k:
            v[f"gx{k}"] = take(f"Bx{k}")
            g = [v[f"g{k}"], v[f"gx{k}"]]
        else:
            g = [after(v["g0"])]
        v[f"i{k}"], send = call(in_kernel, [*g, v["wh"], v["wl"]], [f32(part, rows)] * 2)
        give(f"Dc{k}", send)
        return send

    def step_dc(k):
        total = v[f"i{k}"] + take(f"Dc{k}")
        v[f"i{k}"] = total[:slab]
        give(f"Dy{k}", total[slab:])
        return total

    def step_dy(k):
        v[f"i{k}"] = v[f"i{k}"] + take(f"Dy{k}")
        give(f"Dz{k}", v[f"i{k}"])
        return v[f"i{k}"]

    def step_dz(k):
        v[f"i{k}"] = take(f"Dz{k}")
        return v[f"i{k}"]

    def step_a(k):
        v[f"x{k}"] = take(f"A{k}")
        give(f"Ay{k}", v[f"x{k}"])
        return v[f"x{k}"]

    def step_ay(k):
        v[f"x{k}"] = jnp.concatenate([v[f"x{k}"], take(f"Ay{k}")], axis=0)
        give(f"Ac{k}", v[f"x{k}"])
        return v[f"x{k}"]

    def step_out(k):
        if k:
            v[f"xc{k}"] = take(f"Ac{k}")
            x = [v[f"x{k}"], v[f"xc{k}"]]
        else:
            x = [after(v["x0"])]
        v[f"o{k}"], send = call(out_kernel, [*x, v["wh"], v["wl"]], [f32(half, cols)] * 2)
        give(f"Cx{k}", send)
        return send

    def step_cx(k):
        v[f"o{k}"] = v[f"o{k}"] + take(f"Cx{k}")
        give(f"C{k}", v[f"o{k}"])
        return v[f"o{k}"]

    def step_c2(_):
        a, b = after(got["Cx2"], got["C3"])
        v["o2"] = v["o2"] + a + b
        give("C2", v["o2"])
        return v["o2"]

    def step_grad():
        xs = [v["x0"], *(v[f"{q}{k}"] for k in range(1, dp) for q in ("x", "xc"))]
        gs = [v["g0"], *(v[f"{q}{k}"] for k in range(1, dp) for q in ("g", "gx"))]
        xs[0] = after(xs[0])
        v["new"] = call(
            grad_kernel,
            [*xs, *gs, weight, moment_mean, moment_square],
            [f32(rows, cols)] * 3,
            far=4 * dp + 1,
            far_outs=3,
            limit=40 << 20,
            scratch=[
                pltpu.VMEM((dp, tokens, rows), F32),
                pltpu.VMEM((dp, tokens, cols), F32),
                pltpu.VMEM((3, rows, cols), F32),
                pltpu.VMEM((rows, cols), F32),
                pltpu.SemaphoreType.DMA((4 * dp,)),
                pltpu.SemaphoreType.DMA((3,)),
                pltpu.SemaphoreType.DMA((12,)),
            ],
        )
        return v["new"][0]

    def step_fin():
        a, b = after(got["C1"], got["C2"])
        out = v["o0"] + a + b
        low = lax.axis_index("col") % 2
        v["out"] = jnp.where(low == 0, out, jnp.concatenate([out[slab:], out[:slab]], axis=0))
        return v["out"]

    steps = {"sg": step_sg, "sx": step_sx, "own": step_own, "grad": step_grad, "fin": step_fin}
    families = {"b": step_b, "in": step_in, "dc": step_dc, "dy": step_dy, "dz": step_dz}
    families |= {"a": step_a, "ay": step_ay, "out": step_out, "cx": step_cx, "c": step_c2}
    done = set()
    for name in ORDER.split():
        step = steps.get(name)
        mark(step() if step else families[name[:-1]](int(name[-1])))
        done.add(name)
        for p in list(ready):
            if HOLD.get(p, name) in done:
                x = ready.pop(p)
                if p in permutes and permutes[p][1]:
                    with jax.named_scope(p):
                        got[p] = swap(after(x) if p in HOLD else x, *permutes[p])

    in_grad = jnp.zeros((slab, dp * rows), F32)
    d = lax.axis_index("dp")
    for k in range(dp):
        in_grad = lax.dynamic_update_slice(in_grad, v[f"i{k}"], (0, (d ^ k) * rows))
    return (v["out"], in_grad, *v["new"])


def solution(mesh):
    specs = (P("dp", "row"), P("dp", "col"), *[P(("row", "dp"), "col")] * 3)
    out_specs = (P(("dp", "row"), "col"), P(("dp", "col"), "row"), *[P(("row", "dp"), "col")] * 3)

    def step(inputs, out_grad, weight, moment_mean, moment_square):
        dp, row, col = (mesh.shape[a] for a in ("dp", "row", "col"))
        tokens = inputs.shape[0] // dp
        rows, cols = weight.shape[0] // (row * dp), weight.shape[1] // col
        pairs = dp == 4 and row == 2 and col == 4
        lighter = tokens * (rows // col + cols // row) < rows * cols
        plan = keep_weight if pairs and lighter else gather_weight
        return jax.shard_map(plan, mesh=mesh, in_specs=specs, out_specs=out_specs, check_vma=False)(
            inputs, out_grad, weight, moment_mean, moment_square
        )

    return step
```

```python
import functools
import math

import jax
import jax.numpy as jnp
from jax import lax
from jax.experimental import pallas as pl
from jax.experimental.pallas import tpu as pltpu
from jax.sharding import PartitionSpec as P

STEP = 10
F32 = jnp.float32
BF16 = jnp.bfloat16
VMEM = pl.BlockSpec(memory_space=pltpu.VMEM)
HBM = pl.BlockSpec(memory_space=pltpu.HBM)
NN = (((1,), (0,)), ((), ()))
NT = (((1,), (1,)), ((), ()))
TN = (((0,), (0,)), ((), ()))


def adamw_update(weight, moment_mean, moment_square, gradient):
    new_mean = 0.9 * moment_mean + 0.1 * gradient
    new_square = 0.95 * moment_square + 0.05 * gradient * gradient
    mean_hat = new_mean * (1.0 / (1.0 - 0.9**STEP))
    square_hat = new_square * (1.0 / (1.0 - 0.95**STEP))
    new_weight = weight - 0.02 * (mean_hat / (jnp.sqrt(square_hat) + 1e-08) + 0.1 * weight)
    return (new_weight, new_mean, new_square)


ORDER = " ".join(
    (
        "top sx sg g0",
        "own out0 in0 a3",
        "b1 cx0 out3 b2",
        "a1 in1 in2 out1",
        "grad1 b3 a2 dy2",
        "cx3 grad0 dy1 in3",
        "out2 dz2 grad2 grad3",
        "c2 dz1 dy3 adam",
        "cx1 all fin dz3",
        "dy0",
    )
)
HOLD = {"Gr": "dy3", "Dy3": "dz2", "A1": "a3", "Dy1": "b3", "Dy0": "b2", "B2": "out0"}


def gather_weight(inputs, out_grad, weight, moment_mean, moment_square):
    highest = lax.Precision.HIGHEST
    whole = lax.all_gather(weight, "dp", axis=0, tiled=True)
    partial_out = jnp.dot(inputs, whole, precision=highest, preferred_element_type=F32)
    partial_in = lax.dot_general(out_grad, whole, NT, precision=highest, preferred_element_type=F32)
    outputs = lax.psum_scatter(partial_out, "row", scatter_dimension=0, tiled=True)
    in_grad = lax.psum_scatter(partial_in, "col", scatter_dimension=0, tiled=True)
    factor = 1.0 / math.sqrt(inputs.shape[0] * lax.axis_size("dp"))
    product = lax.dot_general(inputs, out_grad, TN, precision=highest, preferred_element_type=F32)
    gradient = lax.psum_scatter(product, "dp", scatter_dimension=0, tiled=True) * factor
    return (outputs, in_grad, *adamw_update(weight, moment_mean, moment_square, gradient))


def halves(x):
    hi = x.astype(BF16)
    return hi, (x - hi.astype(F32)).astype(BF16)


def dot3(a, b, dims):
    f = functools.partial(lax.dot_general, dimension_numbers=dims, preferred_element_type=F32)
    return f(a[0], b[0]) + (f(a[0], b[1]) + f(a[1], b[0]))


def call(kernel, ins, outs, scratch=(), far=0, far_outs=0, limit=16 << 20):
    ins = [pltpu.with_memory_space_constraint(a, pltpu.HBM) if i < far else a for i, a in enumerate(ins)]
    return pl.pallas_call(
        kernel,
        out_shape=tuple(pltpu.HBM(o.shape, o.dtype) if i < far_outs else o for i, o in enumerate(outs)),
        in_specs=[HBM if i < far else VMEM for i in range(len(ins))],
        out_specs=tuple(HBM if i < far_outs else VMEM for i in range(len(outs))),
        scratch_shapes=list(scratch),
        compiler_params=pltpu.CompilerParams(vmem_limit_bytes=limit),
        cost_estimate=pl.CostEstimate(flops=1000, bytes_accessed=1000, transcendentals=0),
    )(*ins)


def f32(*shape):
    return jax.ShapeDtypeStruct(shape, F32)


def b16(*shape):
    return jax.ShapeDtypeStruct(shape, BF16)


def doubling(n):
    bits, order = [], [0]
    while 1 << len(bits) < n:
        bits.insert(0, 1 << len(bits))
    for bit in bits:
        order = order + [o ^ bit for o in order]
    return bits, order


def swap(x, axis, bit):
    n = lax.axis_size(axis)
    return lax.ppermute(x, axis, [(i, i ^ bit) for i in range(n)])


def keep_weight(inputs, out_grad, weight, moment_mean, moment_square):
    dp, row, col = (lax.axis_size(a) for a in ("dp", "row", "col"))
    tokens, rows, cols = inputs.shape[0], weight.shape[0], weight.shape[1]
    slab, half, part = tokens // col, tokens // row, tokens // 2
    col_bits, order = doubling(col)
    near, far = col_bits[1], col_bits[0]
    last = []

    def after(*xs):
        out = lax.optimization_barrier((*xs, *last))[: len(xs)] if last else xs
        return out[0] if len(xs) == 1 else out

    def mark(*ys):
        last[:] = ys

    mine = [0, far]

    def send_g(g_ref, keep, send, sem):
        c = lax.axis_index("col")
        copies = []
        for j, at in enumerate([*mine, *(o ^ near for o in mine)]):
            src = g_ref.at[pl.ds(pl.multiple_of((c ^ at) * slab, slab), slab), :]
            to = (keep if j < 2 else send).at[pl.ds(j % 2 * slab, slab), :]
            copies.append(pltpu.make_async_copy(src, to, sem.at[j]))
        for cp in copies:
            cp.start()
        for cp in copies:
            cp.wait()

    def send_x(x_ref, *refs):
        outs, own, sem = refs[: dp - 1], refs[dp - 1], refs[dp]
        d, c = lax.axis_index("dp"), lax.axis_index("col")
        copies = []
        for k in range(1, dp):
            src = x_ref.at[pl.ds(pl.multiple_of(c * slab, slab), slab), pl.ds(pl.multiple_of((d ^ k) * rows, rows), rows)]
            copies.append(pltpu.make_async_copy(src, outs[k - 1], sem.at[k - 1]))
        for j, at in enumerate(mine):
            src = x_ref.at[pl.ds(pl.multiple_of((c ^ at) * slab, slab), slab), pl.ds(pl.multiple_of(d * rows, rows), rows)]
            copies.append(pltpu.make_async_copy(src, own.at[pl.ds(j * slab, slab), :], sem.at[dp - 1 + j]))
        for cp in copies:
            cp.start()
        for cp in copies:
            cp.wait()

    def by_core(a, b):
        low = lax.axis_index("col") % 2 == 0
        return jnp.where(low, a, b), jnp.where(low, b, a)

    def join_g(a_ref, b_ref, whole, part_ref):
        first, second = by_core(a_ref[...], b_ref[...])
        whole[:, :cols] = first
        whole[:, cols:] = second
        r = lax.axis_index("row")
        part_ref[:, :cols] = jnp.where(r == 0, first[:slab], first[slab:])
        part_ref[:, cols:] = jnp.where(r == 0, second[:slab], second[slab:])

    def own_weight(a_ref, b_ref, wh, wl, th, tl):
        for i, w in enumerate(by_core(a_ref[...], b_ref[...])):
            at = slice(i * cols, (i + 1) * cols)
            wh[:, at], wl[:, at] = halves(w)
            th[at, :], tl[at, :] = halves(w.T)

    def by_row(g):
        if len(g) == 1:
            return g[0][...]
        r = lax.axis_index("row")
        a, b = g[0][...], g[1][...]
        return jnp.concatenate([jnp.where(r == 0, a, b), jnp.where(r == 0, b, a)], axis=0)

    def in_kernel(*refs):
        g, (th, tl, keep, send) = refs[:-4], refs[-4:]
        p = dot3(halves(by_row(g)), (th[...], tl[...]), NN)
        keep[...], send[...] = p[:slab], p[slab:]

    def out_kernel(*refs):
        xs, (wh, wl, keep, send) = refs[:-4], refs[-4:]
        kept = (lax.axis_index("col") // (col // row)) ^ lax.axis_index("row")
        x = xs[0][...] if len(xs) == 1 else jnp.concatenate([x[...] for x in xs], axis=0)
        o = dot3(halves(x), (wh[...], wl[...]), NN)
        a, b = o[:slab], o[slab:]
        keep[...] = jnp.where(kept == 0, a, b)
        send[...] = jnp.where(kept == 0, b, a)

    factor = 1.0 / math.sqrt(tokens * dp)

    def grad_kernel(nx, ng, last_one, *refs):
        x, g = refs[:nx], refs[nx : nx + ng]
        before, outs = (refs[nx + ng : -2], refs[-2:]) if last_one else (refs[nx + ng : -1], refs[-1:])
        x = x[0][...] if nx == 1 else jnp.concatenate([v[...] for v in x], axis=0)
        total = dot3(halves(x), halves(by_row(g)), TN)
        if before:
            total = before[0][...] + total
        if last_one:
            low = lax.axis_index("col") % 2 == 0
            a, b = total[:, :cols], total[:, cols:]
            outs[0][...] = jnp.where(low, a, b)
            outs[1][...] = jnp.where(low, b, a)
        else:
            outs[0][...] = total

    def adam_kernel(w_ref, m_ref, s_ref, mine_ref, other_ref, nw_ref, nm_ref, ns_ref, state, in_sem, out_sem):
        chunks = 4
        size = rows // chunks
        loads, sends = [], []
        for i in range(chunks):
            at = pl.ds(i * size, size)
            for q, ref in enumerate((w_ref, m_ref, s_ref)):
                loads.append(pltpu.make_async_copy(ref.at[at, :], state.at[q, at, :], in_sem.at[3 * i + q]))
                loads[-1].start()
        for i in range(chunks):
            at = pl.ds(i * size, size)
            for q in range(3):
                loads[3 * i + q].wait()
            gradient = (mine_ref[at, :] + other_ref[at, :]) * factor
            new = adamw_update(state[0, at, :], state[1, at, :], state[2, at, :], gradient)
            for q, ref in enumerate((nw_ref, nm_ref, ns_ref)):
                state[q, at, :] = new[q]
                sends.append(pltpu.make_async_copy(state.at[q, at, :], ref.at[at, :], out_sem.at[3 * i + q]))
                sends[-1].start()
        for cp in sends:
            cp.wait()

    def add_kernel(*refs):
        refs[-1][...] = sum((r[...] for r in refs[1:-1]), start=refs[0][...])

    def out_split_kernel(a_ref, b_ref, c_ref, keep, send):
        total = a_ref[...] + b_ref[...] + c_ref[...]
        low = lax.axis_index("col") % 2 == 0
        keep[...] = jnp.where(low, total[:, :cols], total[:, cols:])
        send[...] = jnp.where(low, total[:, cols:], total[:, :cols])

    def out_order_kernel(a_ref, b_ref, o_ref):
        o_ref[:slab, :], o_ref[slab:, :] = by_core(a_ref[...], b_ref[...])

    def in_order_kernel(*refs):
        pieces, o_ref, sem = refs[:dp], refs[dp], refs[dp + 1]
        d = lax.axis_index("dp")
        copies = []
        for k, piece in enumerate(pieces):
            to = pl.ds(pl.multiple_of((d ^ k) * rows, rows), rows)
            copies.append(pltpu.make_async_copy(piece, o_ref.at[:, to], sem.at[k]))
            copies[-1].start()
        for cp in copies:
            cp.wait()

    def add(*xs):
        return call(add_kernel, xs, [f32(*xs[0].shape)])[0]

    permutes = {"B2": ("dp", 2), "B1": ("dp", 1), "B3": ("dp", 1), "C1": ("dp", 1), "C3": ("dp", 1), "C2": ("dp", 2)}
    for k in range(dp):
        permutes |= {f"A{k}": ("dp", k), f"Dz{k}": ("dp", k), f"Bx{k}": ("row", 1), f"Cx{k}": ("row", 1)}
        permutes |= {f"Ay{k}": ("col", far), f"Dy{k}": ("col", far)}
    permutes |= {p: ("col", near) for p in ("Gc", "Wc", "Oc", "Gr")}
    ready, sent, got, v = {}, {}, {}, {}

    def take(name):
        return after(got[name])

    def give(name, x):
        ready[name] = x

    def step_top():
        give("Wc", weight)
        return None

    def step_sg():
        v["gk"], send = call(send_g, [after(out_grad)], [f32(part, cols)] * 2, far=1, scratch=[pltpu.SemaphoreType.DMA((4,))])
        give("Gc", send)
        return send

    def step_sx():
        *xs, v["x0"] = call(
            send_x,
            [after(inputs)],
            [f32(slab, rows)] * (dp - 1) + [f32(part, rows)],
            far=1,
            scratch=[pltpu.SemaphoreType.DMA((dp + 1,))],
        )
        for k in range(1, dp):
            give(f"A{k}", xs[k - 1])
        return xs[0]

    def step_g(_):
        v["g0"], send = call(join_g, [v["gk"], take("Gc")], [f32(part, 2 * cols), f32(slab, 2 * cols)])
        give("B2", send)
        give("B1", send)
        return send

    def step_own():
        v["wh"], v["wl"], v["th"], v["tl"] = call(
            own_weight, [weight, take("Wc")], [b16(rows, 2 * cols)] * 2 + [b16(2 * cols, rows)] * 2, limit=24 << 20
        )
        return v["wh"]

    def step_b(k):
        v[f"g{k}"] = take(f"B{k}")
        if k == 2:
            give("B3", v["g2"])
        give(f"Bx{k}", v[f"g{k}"])
        return v[f"g{k}"]

    def step_in(k):
        if k:
            v[f"gx{k}"] = take(f"Bx{k}")
            g = [v[f"g{k}"], v[f"gx{k}"]]
        else:
            g = [after(v["g0"])]
        v[f"i{k}"], send = call(in_kernel, [*g, v["th"], v["tl"]], [f32(slab, rows)] * 2)
        give(f"Dy{k}", send)
        return send

    def step_dy(k):
        v[f"i{k}"] = add(v[f"i{k}"], take(f"Dy{k}"))
        give(f"Dz{k}", v[f"i{k}"])
        return v[f"i{k}"]

    def step_dz(k):
        v[f"i{k}"] = take(f"Dz{k}")
        return v[f"i{k}"]

    def step_a(k):
        v[f"x{k}"] = take(f"A{k}")
        give(f"Ay{k}", v[f"x{k}"])
        return v[f"x{k}"]

    def step_out(k):
        if k:
            v[f"xy{k}"] = take(f"Ay{k}")
            x = [v[f"x{k}"], v[f"xy{k}"]]
        else:
            x = [after(v["x0"])]
        v[f"o{k}"], send = call(out_kernel, [*x, v["wh"], v["wl"]], [f32(slab, 2 * cols)] * 2)
        give(f"Cx{k}", send)
        return send

    def step_cx(k):
        v[f"o{k}"] = add(v[f"o{k}"], take(f"Cx{k}"))
        give(f"C{k}", v[f"o{k}"])
        return v[f"o{k}"]

    def step_c2(_):
        a, b = after(got["Cx2"], got["C3"])
        v["o2"] = add(v["o2"], a, b)
        give("C2", v["o2"])
        return v["o2"]

    def step_grad(k):
        x = [v["x0"]] if k == 0 else [v[f"x{k}"], v[f"xy{k}"]]
        g = [v["g0"]] if k == 0 else [v[f"g{k}"], v[f"gx{k}"]]
        before = [v["total"]] if "total" in v else []
        shares.append(k)
        last_one = len(shares) == dp
        x[0] = after(x[0])
        outs = call(
            functools.partial(grad_kernel, len(x), len(g), last_one),
            [*x, *g, *before],
            [f32(rows, cols)] * 2 if last_one else [f32(rows, 2 * cols)],
            limit=24 << 20,
        )
        v["total"] = outs[0]
        if last_one:
            give("Gr", outs[1])
        return outs[-1]

    def step_adam():
        v["new"] = call(
            adam_kernel,
            [weight, moment_mean, moment_square, v["total"], take("Gr")],
            [f32(rows, cols)] * 3,
            far=3,
            far_outs=3,
            scratch=[pltpu.VMEM((3, rows, cols), F32), pltpu.SemaphoreType.DMA((12,)), pltpu.SemaphoreType.DMA((12,))],
        )
        return v["new"][0]

    def step_all():
        a, b = after(got["C1"], got["C2"])
        v["ok"], send = call(out_split_kernel, [v["o0"], a, b], [f32(slab, cols)] * 2)
        give("Oc", send)
        return send

    def step_fin():
        (v["out"],) = call(out_order_kernel, [v["ok"], take("Oc")], [f32(half, cols)])
        return v["out"]

    shares = []
    steps = {"top": step_top, "sg": step_sg, "sx": step_sx, "own": step_own, "adam": step_adam, "fin": step_fin, "all": step_all}
    families = {"b": step_b, "in": step_in, "dy": step_dy, "dz": step_dz}
    families |= {"grad": step_grad, "a": step_a, "g": step_g, "out": step_out, "cx": step_cx, "c": step_c2}
    done = set()
    for name in ORDER.split():
        step = steps.get(name)
        result = step() if step else families[name[:-1]](int(name[-1]))
        if result is not None:
            mark(result)
        done.add(name)
        for p in list(ready):
            if HOLD.get(p, name) in done:
                x = ready.pop(p)
                if p in permutes and permutes[p][1]:
                    with jax.named_scope(p):
                        got[p] = swap(after(x) if p in HOLD else x, *permutes[p])

    (in_grad,) = call(
        in_order_kernel,
        [after(v["i0"]), *(v[f"i{k}"] for k in range(1, dp))],
        [f32(slab, dp * rows)],
        far_outs=1,
        scratch=[pltpu.SemaphoreType.DMA((dp,))],
    )
    return (v["out"], in_grad, *v["new"])


def solution(mesh):
    specs = (P("dp", "row"), P("dp", "col"), *[P(("row", "dp"), "col")] * 3)
    out_specs = (P(("dp", "row"), "col"), P(("dp", "col"), "row"), *[P(("row", "dp"), "col")] * 3)

    def step(inputs, out_grad, weight, moment_mean, moment_square):
        dp, row, col = (mesh.shape[a] for a in ("dp", "row", "col"))
        tokens = inputs.shape[0] // dp
        rows, cols = weight.shape[0] // (row * dp), weight.shape[1] // col
        pairs = dp == 4 and row == 2 and col == 4
        lighter = tokens * (rows // col + cols // row) < rows * cols
        plan = keep_weight if pairs and lighter else gather_weight
        return jax.shard_map(plan, mesh=mesh, in_specs=specs, out_specs=out_specs, check_vma=False)(
            inputs, out_grad, weight, moment_mean, moment_square
        )

    return step
```
